32 devices in a mesh: blk: 8 (over z, y), aux: 4 (over x, core).
Axes of the slice: x: 2, y: 2, z: 4, core: 2. Of those that a mesh axis runs over, the one named last changes fastest.
Arguments:
- ints3c: bfloat16 [8, 4096, 3, 512], P('aux', 'blk'), may hold values from -0.25 to 0.25
- coef: bfloat16 [4096, 256], P('blk'), may hold values from -6 to 6
- tile_mask: int32 [8, 3, 4], P('blk'), may hold values 0 or 1
Outputs:
- band: float32 [4096, 3, 512], P('blk', None, 'aux')
The draws below stay inside these ranges and needn't reach their ends.
All inputs are finite; a program needn't handle non-finite values. No bound on the sum of `tile_mask` on one device may be relied on, other than what follows from the above.
Results may differ from the reference program's by a relative error of at most 0.0016.
Values may be sent and summed in bfloat16 or wider, within the bound.
A program may use at most 64 MiB of HBM per device.

```python
import jax
import jax.numpy as jnp
from jax import lax

BAS_DEV = 512
OCC_DEV = 256
TILES = 4
NBAS = 4096
NAUX = 8
N_BLK = 8


def place_ends(entries, stream_key, least, high):
    longest = entries.shape.index(max(entries.shape))
    spots = []
    for shift in (0, 1):
        where = [jax.random.randint(jax.random.fold_in(stream_key, axis), (), 0, length) for axis, length in enumerate(entries.shape)]
        where[longest] = (where[longest] + shift) % entries.shape[longest]
        spots.append(tuple(where))
    return entries.at[spots[0]].set(least).at[spots[1]].set(high)


def steps_of(rng, extent, pieces, least, largest):
    level = 1.0
    for position, parts in pieces:
        heights = jax.random.uniform(jax.random.fold_in(jax.random.fold_in(rng, 6), position), (parts,), jnp.float32, least / len(pieces), largest / len(pieces))
        level = level * jnp.repeat(jnp.exp(heights), extent[position] // parts).reshape((-1,) + (1,) * (len(extent) - 1 - position))
    return level


def noise(rng, extent, deviation, limit, pieces=(), held_as=jnp.bfloat16):
    drawn = jax.random.normal(rng, extent, jnp.float32) * deviation
    if len(pieces) > 0:
        drawn = steps_of(rng, extent, pieces, -0.22, 0.18) * drawn
    return jnp.clip(drawn, min=-limit, max=limit).astype(held_as)


def setup_inputs(seed: int = 0) -> dict:
    splits = jax.random.split(jax.random.key(seed), 4)
    return {
        "ints3c": noise(splits[0], (NAUX, NBAS, 3, BAS_DEV), BAS_DEV ** -0.5, 0.25, ((0, 4), (1, 8))),
        "coef": noise(splits[1], (NBAS, OCC_DEV), 1.0, 6.0, ((0, 8),)),
        "tile_mask": place_ends((jax.random.randint(splits[2], (N_BLK, 3, TILES), 0, 4) < 3).astype(jnp.int32), jax.random.fold_in(splits[2], 1), 0, 1),
    }


def reference(ints3c, coef, tile_mask):
    ints = jnp.moveaxis(ints3c.reshape(NAUX, N_BLK, BAS_DEV, 3, BAS_DEV), 1, 0)
    blocks = coef.reshape(N_BLK, BAS_DEV, OCC_DEV)
    windows = jnp.stack([jnp.roll(blocks, 1, 0), blocks, jnp.roll(blocks, -1, 0)], axis=1)
    weights = jnp.repeat(tile_mask.astype(jnp.float32), BAS_DEV // TILES, axis=2)

    def one_block(args):
        block_ints, block_coef, block_weights = args
        prod = jnp.einsum('pmkn,kni->pmki', block_ints.astype(jnp.float32), block_coef.astype(jnp.float32))
        return (prod * jnp.transpose(block_weights)[None, :, :, None]).astype(jnp.bfloat16)

    half = lax.map(one_block, (ints, windows, weights))
    scale = (NAUX * 3 * OCC_DEV) ** -0.5

    def band_block(index):
        own = half[index].astype(jnp.float32)
        after = half[(index + 1) % N_BLK].astype(jnp.float32)
        before = half[(index + N_BLK - 1) % N_BLK].astype(jnp.float32)
        diag = jnp.einsum('pmki,plki->ml', own, own)
        upper = jnp.einsum('pmki,plki->ml', own[:, :, 1:], after[:, :, :2])
        lower = jnp.einsum('pmki,plki->ml', own[:, :, :2], before[:, :, 1:])
        return jnp.stack([lower, diag, upper], axis=1) * scale

    band = lax.map(band_block, jnp.arange(N_BLK, dtype=jnp.int32))
    return band.reshape(NBAS, 3, BAS_DEV)
```

```python
import functools

import jax
import jax.numpy as jnp
from jax import lax
from jax.experimental import pallas as pl
from jax.experimental.pallas import tpu as pltpu
from jax.sharding import PartitionSpec as P

MESH = pl.DeviceIdType.MESH
F32 = jnp.float32
BF16 = jnp.bfloat16


def dot(a, b):
    return jnp.dot(a, b, preferred_element_type=F32)


def dot_t(a, b):
    return lax.dot_general(a, b, (((1,), (1,)), ((), ())), preferred_element_type=F32)


def kernel(n, na, scale, mask_ref, coef_ref, ints_ref, out_ref, ints, cwin, hs, rh, diag, dsend, drecv,
           up, usend, urecv, lrecv, fsend, frecv, load_sem, c_send, c_recv, g_send, g_recv, h_send,
           h_recv, d_send, d_recv, u_send, u_recv, l_send, l_recv, f_send, f_recv):
    b = lax.axis_index("blk")
    a = lax.axis_index("aux")
    aux_p, _, rows, _ = ints_ref.shape
    occ = coef_ref.shape[1]
    tiles = mask_ref.shape[2]
    tile = rows // tiles
    part = rows // na
    nxt = lax.rem(b + 1, n)
    prv = lax.rem(b + n - 1, n)
    mates = [lax.rem(a + r, na) for r in range(1, na)]

    def remote(src, dst, ssem, rsem, to):
        return pltpu.make_async_remote_copy(
            src_ref=src, dst_ref=dst, send_sem=ssem, recv_sem=rsem, device_id=to, device_id_type=MESH)

    barrier = pltpu.get_barrier_semaphore()
    for to in [(nxt, a), (prv, a)] + [(b, m) for m in mates]:
        pl.semaphore_signal(barrier, inc=1, device_id=to, device_id_type=MESH)

    loads = {}
    for k in (1, 0, 2):
        for p in range(aux_p):
            loads[k, p] = pltpu.make_async_copy(
                ints_ref.at[p, k], ints.at[k, p], load_sem.at[k, p])
            loads[k, p].start()

    def transform(k, window, t0, t1):
        for p in range(aux_p):
            if t0 == 0:
                loads[k, p].wait()
            prod = dot(ints[k, p, t0 * tile:t1 * tile, :], window)
            for t in range(t0, t1):
                weight = mask_ref[0, k, t].astype(F32)
                piece = prod[(t - t0) * tile:(t - t0 + 1) * tile, :] * weight
                hs[k, t * tile:(t + 1) * tile, p * occ:(p + 1) * occ] = piece.astype(BF16)

    pl.semaphore_wait(barrier, 2 + len(mates))

    mine = pl.ds(pl.multiple_of(a * part, part), part)
    coef_out = []
    for side, to in ((0, (nxt, a)), (1, (prv, a))):
        copy = remote(coef_ref.at[mine], cwin.at[side, mine], c_send.at[side], c_recv.at[side], to)
        copy.start()
        coef_out.append(copy)

    half_out = []

    def send_half(k, j):
        cut = pl.ds(j * part, part)
        copy = remote(hs.at[k, cut], rh.at[k, cut], h_send.at[k, j], h_recv.at[k, j], (prv, a))
        copy.start()
        half_out.append(copy)

    transform(1, coef_ref[...], 0, tiles)
    for j in range(na):
        send_half(1, j)

    gather_out = []
    for side in (0, 1):
        coef_out[side].wait_recv()
        for r, m in enumerate(mates):
            copy = remote(cwin.at[side, mine], cwin.at[side, mine], g_send.at[side, r],
                          g_recv.at[side, r], (b, m))
            copy.start()
            gather_out.append(copy)

    def gathered(side):
        for r in range(na - 1):
            src = lax.rem(a + na - r - 1, na)
            their = pl.ds(pl.multiple_of(src * part, part), part)
            remote(cwin.at[side, their], cwin.at[side, their], g_send.at[side, r],
                   g_recv.at[side, r], (b, src)).wait_recv()

    gathered(0)
    per = tiles // na
    for j in range(na):
        transform(0, cwin[0], j * per, (j + 1) * per)
        send_half(0, j)
    gathered(1)
    transform(2, cwin[1], 0, tiles)

    diag[...] = dot_t(hs[0], hs[0]) + dot_t(hs[1], hs[1]) + dot_t(hs[2], hs[2])
    for c in range(na):
        dsend[c] = diag[:, c * part:(c + 1) * part].astype(BF16)
    diag_out = []
    for r, m in enumerate(mates):
        copy = remote(dsend.at[m], drecv.at[r], d_send.at[r], d_recv.at[r], (b, m))
        copy.start()
        diag_out.append(copy)

    for j in range(na):
        half_out[j].wait_recv()
    up[...] = dot_t(hs[2], rh[1])

    low_out = {}
    final_out = []

    def reduce_lower(j):
        cols = pl.ds(j * part, part)
        total = up[mine, cols]
        for r in range(na - 1):
            low_out[j, r].wait_recv()
            total = total + lrecv[j, r].astype(F32)
        fsend[cols, :] = total.T.astype(BF16)
        copy = remote(fsend.at[cols], frecv.at[cols], f_send.at[j], f_recv.at[j], (nxt, a))
        copy.start()
        final_out.append(copy)

    def upper_copy(j, slot):
        return remote(usend.at[j], urecv.at[slot], u_send.at[j], u_recv.at[slot], (b, j))

    for j in range(na):
        half_out[na + j].wait_recv()
        cols = pl.ds(j * part, part)
        value = up[:, cols] + dot_t(hs[1], rh[0, cols, :])
        up[:, cols] = value
        usend[j] = value.astype(BF16)
        for r, m in enumerate(mates):
            take = pl.ds(pl.multiple_of(m * part, part), part)
            low_out[j, r] = remote(usend.at[j, take], lrecv.at[j, r], l_send.at[j, r],
                                   l_recv.at[j, r], (b, m))
            low_out[j, r].start()

        @pl.when(a != j)
        def _():
            upper_copy(j, lax.rem(j - a + na, na) - 1).start()

        if j > 0:
            reduce_lower(j - 1)
    reduce_lower(na - 1)

    total = diag[:, mine]
    for r in range(na - 1):
        diag_out[r].wait_recv()
        total = total + drecv[r].astype(F32)
    out_ref[1] = total * scale

    total = up[:, mine]
    for r in range(na - 1):
        remote(usend.at[0], urecv.at[r], u_send.at[0], u_recv.at[r], (b, mates[r])).wait_recv()
        total = total + urecv[r].astype(F32)
    out_ref[2] = total * scale

    for j in range(na):
        final_out[j].wait_recv()
    out_ref[0] = frecv[...].astype(F32) * scale

    for copy in coef_out + half_out + gather_out + diag_out + list(low_out.values()) + final_out:
        copy.wait_send()
    for j in range(na):
        @pl.when(a != j)
        def _():
            upper_copy(j, lax.rem(j - a + na, na) - 1).wait_send()


def body(n, na, ints3c, coef, tile_mask):
    ints = jnp.transpose(ints3c, (0, 2, 1, 3))
    aux_p, kk, rows, cols = ints.shape
    occ = coef.shape[1]
    part = rows // na
    scale = (na * aux_p * 3 * occ) ** (-0.5)
    dma = pltpu.SemaphoreType.DMA
    out = pl.pallas_call(
        functools.partial(kernel, n, na, scale),
        out_shape=jax.ShapeDtypeStruct((3, rows, part), F32),
        in_specs=[
            pl.BlockSpec(memory_space=pltpu.SMEM),
            pl.BlockSpec(memory_space=pltpu.VMEM),
            pl.BlockSpec(memory_space=pl.ANY),
        ],
        out_specs=pl.BlockSpec(memory_space=pltpu.VMEM),
        scratch_shapes=[
            pltpu.VMEM((3, aux_p, rows, cols), BF16),
            pltpu.VMEM((2, rows, occ), BF16),
            pltpu.VMEM((3, rows, aux_p * occ), BF16),
            pltpu.VMEM((2, rows, aux_p * occ), BF16),
            pltpu.VMEM((rows, rows), F32),
            pltpu.VMEM((na, rows, part), BF16),
            pltpu.VMEM((na - 1, rows, part), BF16),
            pltpu.VMEM((rows, rows), F32),
            pltpu.VMEM((na, rows, part), BF16),
            pltpu.VMEM((na - 1, rows, part), BF16),
            pltpu.VMEM((na, na - 1, part, part), BF16),
            pltpu.VMEM((rows, part), BF16),
            pltpu.VMEM((rows, part), BF16),
            dma((3, aux_p)),
            dma((2,)), dma((2,)),
            dma((2, na - 1)), dma((2, na - 1)),
            dma((2, na)), dma((2, na)),
            dma((na - 1,)), dma((na - 1,)),
            dma((na,)), dma((na - 1,)),
            dma((na, na - 1)), dma((na, na - 1)),
            dma((na,)), dma((na,)),
        ],
        compiler_params=pltpu.CompilerParams(
            collective_id=0, has_side_effects=True, vmem_limit_bytes=40 * 1024 * 1024),
        cost_estimate=pl.CostEstimate(
            flops=2 * rows * rows * occ * aux_p * 8, bytes_accessed=ints.size * 2 + rows * rows * 12,
            transcendentals=0),
    )(tile_mask, coef, ints)
    return jnp.transpose(out, (1, 0, 2))


def solution(mesh):
    placed = (P("aux", "blk", None, None), P("blk", None), P("blk", None, None))
    return jax.shard_map(
        functools.partial(body, mesh.shape["blk"], mesh.shape["aux"]),
        mesh=mesh, in_specs=placed, out_specs=P("blk", None, "aux"), check_vma=False,
    )
```

```python
import functools

import jax
import jax.numpy as jnp
from jax import lax
from jax.experimental import pallas as pl
from jax.experimental.pallas import tpu as pltpu
from jax.sharding import PartitionSpec as P

MESH = pl.DeviceIdType.MESH
F32 = jnp.float32
BF16 = jnp.bfloat16


def dot(a, b):
    return jnp.dot(a, b, preferred_element_type=F32)


def dot_t(a, b):
    return lax.dot_general(a, b, (((1,), (1,)), ((), ())), preferred_element_type=F32)


def kernel(n, na, scale, mask_ref, coef_ref, ints_ref, out_ref, coef_vmem, ints, cwin, hs, rh, diag, dsend, drecv,
           up, usend, urecv, lrecv, fsend, frecv, coef_sem, load_sem, c_send, c_recv, g_send, g_recv, h_send,
           h_recv, d_send, d_recv, u_send, u_recv, l_send, l_recv, f_send, f_recv):
    b = lax.axis_index("blk")
    a = lax.axis_index("aux")
    aux_p, _, rows, _ = ints_ref.shape
    occ = coef_ref.shape[1]
    tiles = mask_ref.shape[2]
    tile = rows // tiles
    part = rows // na
    nxt = lax.rem(b + 1, n)
    prv = lax.rem(b + n - 1, n)
    far = lax.rem(a + na // 2, na)
    near = a + 1 - 2 * lax.rem(a, 2)
    mates = [lax.rem(a + r, na) for r in range(1, na)]

    def remote(src, dst, ssem, rsem, to):
        return pltpu.make_async_remote_copy(
            src_ref=src, dst_ref=dst, send_sem=ssem, recv_sem=rsem, device_id=to, device_id_type=MESH)

    barrier = pltpu.get_barrier_semaphore()
    for to in [(nxt, a), (prv, a)] + [(b, m) for m in mates]:
        pl.semaphore_signal(barrier, inc=1, device_id=to, device_id_type=MESH)

    coef_load = pltpu.make_async_copy(coef_ref, coef_vmem, coef_sem)
    coef_load.start()
    loads = {}
    for k in (1, 0, 2):
        for p in range(aux_p):
            loads[k, p] = pltpu.make_async_copy(
                ints_ref.at[p, k], ints.at[k, p], load_sem.at[k, p])
            loads[k, p].start()

    def transform(k, window, t0, t1):
        for p in range(aux_p):
            if t0 == 0:
                loads[k, p].wait()
            prod = dot(ints[k, p, t0 * tile:t1 * tile, :], window[...])
            for t in range(t0, t1):
                weight = mask_ref[0, k, t].astype(F32)
                piece = prod[(t - t0) * tile:(t - t0 + 1) * tile, :] * weight
                hs[k, t * tile:(t + 1) * tile, p * occ:(p + 1) * occ] = piece.astype(BF16)

    coef_load.wait()
    pl.semaphore_wait(barrier, 2 + len(mates))

    mine = pl.ds(pl.multiple_of(a * part, part), part)
    coef_out = []
    for side, to in ((0, (nxt, a)), (1, (prv, a))):
        copy = remote(coef_vmem.at[mine], cwin.at[side, mine], c_send.at[side], c_recv.at[side], to)
        copy.start()
        coef_out.append(copy)

    half_out = []

    def send_half(k, j):
        cut = pl.ds(j * part, part)
        copy = remote(hs.at[k, cut], rh.at[k, cut], h_send.at[k, j], h_recv.at[k, j], (prv, a))
        copy.start()
        half_out.append(copy)

    transform(1, coef_vmem, 0, tiles)

    gather_out = {}

    def pass_on(side, r, owner, to):
        cut = pl.ds(pl.multiple_of(owner * part, part), part)
        gather_out[side, r] = remote(cwin.at[side, cut], cwin.at[side, cut], g_send.at[side, r],
                                     g_recv.at[side, r], (b, to))
        gather_out[side, r].start()

    for side in (0, 1):
        coef_out[side].wait_recv()
        pass_on(side, 0, a, far)
        pass_on(side, 1, a, near)
    for j in range(na):
        send_half(1, j)
    for side in (0, 1):
        gather_out[side, 0].wait_recv()
        pass_on(side, 2, far, near)

    def gathered(side):
        gather_out[side, 1].wait_recv()
        gather_out[side, 2].wait_recv()

    gathered(0)
    per = tiles // na
    for j in range(na):
        transform(0, cwin.at[0], j * per, (j + 1) * per)
        send_half(0, j)
    gathered(1)
    transform(2, cwin.at[1], 0, tiles)

    diag[...] = dot_t(hs[0], hs[0]) + dot_t(hs[1], hs[1]) + dot_t(hs[2], hs[2])
    for c in range(na):
        dsend[c] = diag[:, c * part:(c + 1) * part].astype(BF16)
    diag_out = []
    for r, m in enumerate(mates):
        copy = remote(dsend.at[m], drecv.at[r], d_send.at[r], d_recv.at[r], (b, m))
        copy.start()
        diag_out.append(copy)

    for j in range(na):
        half_out[j].wait_recv()
    up[...] = dot_t(hs[2], rh[1])

    low_out = {}
    final_out = []

    def reduce_lower(j):
        cols = pl.ds(j * part, part)
        total = up[mine, cols]
        for r in range(na - 1):
            low_out[j, r].wait_recv()
            total = total + lrecv[j, r].astype(F32)
        fsend[cols, :] = total.T.astype(BF16)
        copy = remote(fsend.at[cols], frecv.at[cols], f_send.at[j], f_recv.at[j], (nxt, a))
        copy.start()
        final_out.append(copy)

    def upper_copy(j, slot):
        return remote(usend.at[j], urecv.at[slot], u_send.at[j], u_recv.at[slot], (b, j))

    for j in range(na):
        half_out[na + j].wait_recv()
        cols = pl.ds(j * part, part)
        value = up[:, cols] + dot_t(hs[1], rh[0, cols, :])
        up[:, cols] = value
        usend[j] = value.astype(BF16)
        for r, m in enumerate(mates):
            take = pl.ds(pl.multiple_of(m * part, part), part)
            low_out[j, r] = remote(usend.at[j, take], lrecv.at[j, r], l_send.at[j, r],
                                   l_recv.at[j, r], (b, m))
            low_out[j, r].start()

        @pl.when(a != j)
        def _():
            upper_copy(j, lax.rem(j - a + na, na) - 1).start()

        if j > 0:
            reduce_lower(j - 1)
    reduce_lower(na - 1)

    total = diag[:, mine]
    for r in range(na - 1):
        diag_out[r].wait_recv()
        total = total + drecv[r].astype(F32)
    out_ref[1] = total * scale

    total = up[:, mine]
    for r in range(na - 1):
        remote(usend.at[0], urecv.at[r], u_send.at[0], u_recv.at[r], (b, mates[r])).wait_recv()
        total = total + urecv[r].astype(F32)
    out_ref[2] = total * scale

    for j in range(na):
        final_out[j].wait_recv()
    out_ref[0] = frecv[...].astype(F32) * scale

    for copy in coef_out + half_out + list(gather_out.values()) + diag_out + list(low_out.values()) + final_out:
        copy.wait_send()
    for j in range(na):
        @pl.when(a != j)
        def _():
            upper_copy(j, lax.rem(j - a + na, na) - 1).wait_send()


def body(n, na, ints3c, coef, tile_mask):
    ints = jnp.transpose(ints3c, (0, 2, 1, 3))
    aux_p, kk, rows, cols = ints.shape
    occ = coef.shape[1]
    part = rows // na
    scale = (na * aux_p * 3 * occ) ** (-0.5)
    dma = pltpu.SemaphoreType.DMA
    out = pl.pallas_call(
        functools.partial(kernel, n, na, scale),
        out_shape=jax.ShapeDtypeStruct((3, rows, part), F32),
        in_specs=[
            pl.BlockSpec(memory_space=pltpu.SMEM),
            pl.BlockSpec(memory_space=pl.ANY),
            pl.BlockSpec(memory_space=pl.ANY),
        ],
        out_specs=pl.BlockSpec(memory_space=pltpu.VMEM),
        scratch_shapes=[
            pltpu.VMEM((rows, occ), BF16),
            pltpu.VMEM((3, aux_p, rows, cols), BF16),
            pltpu.VMEM((2, rows, occ), BF16),
            pltpu.VMEM((3, rows, aux_p * occ), BF16),
            pltpu.VMEM((2, rows, aux_p * occ), BF16),
            pltpu.VMEM((rows, rows), F32),
            pltpu.VMEM((na, rows, part), BF16),
            pltpu.VMEM((na - 1, rows, part), BF16),
            pltpu.VMEM((rows, rows), F32),
            pltpu.VMEM((na, rows, part), BF16),
            pltpu.VMEM((na - 1, rows, part), BF16),
            pltpu.VMEM((na, na - 1, part, part), BF16),
            pltpu.VMEM((rows, part), BF16),
            pltpu.VMEM((rows, part), BF16),
            dma, dma((3, aux_p)),
            dma((2,)), dma((2,)),
            dma((2, 3)), dma((2, 3)),
            dma((2, na)), dma((2, na)),
            dma((na - 1,)), dma((na - 1,)),
            dma((na,)), dma((na - 1,)),
            dma((na, na - 1)), dma((na, na - 1)),
            dma((na,)), dma((na,)),
        ],
        compiler_params=pltpu.CompilerParams(
            collective_id=0, has_side_effects=True, vmem_limit_bytes=40 * 1024 * 1024),
        cost_estimate=pl.CostEstimate(
            flops=2 * rows * rows * occ * aux_p * 8, bytes_accessed=ints.size * 2 + rows * rows * 12,
            transcendentals=0),
    )(tile_mask, coef, ints)
    return jnp.transpose(out, (1, 0, 2))


def solution(mesh):
    placed = (P("aux", "blk", None, None), P("blk", None), P("blk", None, None))
    return jax.shard_map(
        functools.partial(body, mesh.shape["blk"], mesh.shape["aux"]),
        mesh=mesh, in_specs=placed, out_specs=P("blk", None, "aux"), check_vma=False,
    )
```

```python
import functools

import jax
import jax.numpy as jnp
from jax import lax
from jax.experimental import pallas as pl
from jax.experimental.pallas import tpu as pltpu
from jax.sharding import PartitionSpec as P

MESH = pl.DeviceIdType.MESH
F32 = jnp.float32
BF16 = jnp.bfloat16


def dot(a, b):
    return jnp.dot(a, b, preferred_element_type=F32)


def dot_t(a, b):
    return lax.dot_general(a, b, (((1,), (1,)), ((), ())), preferred_element_type=F32)


def kernel(n, na, scale, mask_ref, coef_ref, ints_ref, out_ref, coef_vmem, ints, cwin, hs, rh, diag, dsend, drecv,
           dsend2, drecv2, up, usend, urecv, usend2, urecv2, lrecv, lsend2, lrecv2, fsend, frecv, coef_sem, load_sem, c_send, c_recv, g_send, g_recv, h_send,
           h_recv, d_send, d_recv, u_send, u_recv, l_send, l_recv, f_send, f_recv):
    b = lax.axis_index("blk")
    a = lax.axis_index("aux")
    aux_p, _, rows, _ = ints_ref.shape
    occ = coef_ref.shape[1]
    tiles = mask_ref.shape[2]
    tile = rows // tiles
    part = rows // na
    nxt = lax.rem(b + 1, n)
    prv = lax.rem(b + n - 1, n)
    far = lax.rem(a + na // 2, na)
    near = a + 1 - 2 * lax.rem(a, 2)
    mates = [lax.rem(a + r, na) for r in range(1, na)]

    def remote(src, dst, ssem, rsem, to):
        return pltpu.make_async_remote_copy(
            src_ref=src, dst_ref=dst, send_sem=ssem, recv_sem=rsem, device_id=to, device_id_type=MESH)

    barrier = pltpu.get_barrier_semaphore()
    for to in [(nxt, a), (prv, a)] + [(b, m) for m in mates]:
        pl.semaphore_signal(barrier, inc=1, device_id=to, device_id_type=MESH)

    coef_load = pltpu.make_async_copy(coef_ref, coef_vmem, coef_sem)
    coef_load.start()
    loads = {}
    for k in (1, 0, 2):
        for p in range(aux_p):
            loads[k, p] = pltpu.make_async_copy(
                ints_ref.at[p, k], ints.at[k, p], load_sem.at[k, p])
            loads[k, p].start()

    def transform(k, window, t0, t1):
        for p in range(aux_p):
            if t0 == 0:
                loads[k, p].wait()
            prod = dot(ints[k, p, t0 * tile:t1 * tile, :], window[...])
            for t in range(t0, t1):
                weight = mask_ref[k, 0, t].astype(F32)
                piece = prod[(t - t0) * tile:(t - t0 + 1) * tile, :] * weight
                hs[k, t * tile:(t + 1) * tile, p * occ:(p + 1) * occ] = piece.astype(BF16)

    coef_load.wait()
    pl.semaphore_wait(barrier, 2 + len(mates))

    mine = pl.ds(pl.multiple_of(a * part, part), part)
    coef_out = []
    for side, to in ((0, (nxt, a)), (1, (prv, a))):
        copy = remote(coef_vmem.at[mine], cwin.at[side, mine], c_send.at[side], c_recv.at[side], to)
        copy.start()
        coef_out.append(copy)

    half_out = []

    def send_half(k, j):
        cut = pl.ds(j * part, part)
        copy = remote(hs.at[k, cut], rh.at[k, cut], h_send.at[k, j], h_recv.at[k, j], (prv, a))
        copy.start()
        half_out.append(copy)

    transform(1, coef_vmem, 0, tiles)

    gather_out = {}

    def pass_on(side, r, owner, to):
        cut = pl.ds(pl.multiple_of(owner * part, part), part)
        gather_out[side, r] = remote(cwin.at[side, cut], cwin.at[side, cut], g_send.at[side, r],
                                     g_recv.at[side, r], (b, to))
        gather_out[side, r].start()

    for side in (0, 1):
        coef_out[side].wait_recv()
        pass_on(side, 0, a, far)
        pass_on(side, 1, a, near)
    for j in range(na):
        send_half(1, j)
    for side in (0, 1):
        gather_out[side, 0].wait_recv()
        pass_on(side, 2, far, near)

    def gathered(side):
        gather_out[side, 1].wait_recv()
        gather_out[side, 2].wait_recv()

    gathered(0)
    per = tiles // na
    for j in range(na):
        transform(0, cwin.at[0], j * per, (j + 1) * per)
        send_half(0, j)
    gathered(1)
    transform(2, cwin.at[1], 0, tiles)

    near_far = lax.rem(near + na // 2, na)
    core, x, far_x = lax.rem(a, 2), a // 2, far // 2
    near_core = lax.rem(near, 2)
    far_cols = pl.ds(pl.multiple_of(far * part, part), part)

    diag[...] = dot_t(hs[0], hs[0]) + dot_t(hs[1], hs[1]) + dot_t(hs[2], hs[2])
    for c in range(na):
        dsend[c % 2, c // 2] = diag[:, c * part:(c + 1) * part].astype(BF16)
    diag_near = remote(dsend.at[near_core], drecv, d_send.at[0], d_recv.at[0], (b, near))
    diag_near.start()

    for j in range(na):
        half_out[j].wait_recv()
    up[...] = dot_t(hs[2], rh[1])

    diag_near.wait_recv()
    dsend2[...] = (diag[:, far_cols] + drecv[far_x].astype(F32)).astype(BF16)
    diag_far = remote(dsend2, drecv2, d_send.at[1], d_recv.at[1], (b, far))
    diag_far.start()

    low_near, low_far, final_out = {}, {}, []

    def upper_near(j):
        return remote(usend.at[j], urecv.at[j // 2], u_send.at[j // 2], u_recv.at[j // 2], (b, near))

    upper_far = remote(usend2, urecv2, u_send.at[2], u_recv.at[2], (b, far))

    def compute(j):
        half_out[na + j].wait_recv()
        cols = pl.ds(j * part, part)
        value = up[:, cols] + dot_t(hs[1], rh[0, cols, :])
        up[:, cols] = value
        usend[j] = value.astype(BF16)
        for i, owner in enumerate((near, near_far)):
            take = pl.ds(pl.multiple_of(owner * part, part), part)
            low_near[j, i] = remote(usend.at[j, take], lrecv.at[j, i], l_send.at[j, i],
                                    l_recv.at[j, i], (b, near))
            low_near[j, i].start()

        @pl.when(core != j % 2)
        def _():
            upper_near(j).start()

    def second(j):
        cols = pl.ds(j * part, part)
        low_near[j, 1].wait_recv()
        lsend2[j] = (up[far_cols, cols] + lrecv[j, 1].astype(F32)).astype(BF16)
        low_far[j] = remote(lsend2.at[j], lrecv2.at[j], l_send.at[j, 2], l_recv.at[j, 2], (b, far))
        low_far[j].start()

        @pl.when(far == j)
        def _():
            upper_near(j).wait_recv()
            usend2[...] = (up[:, cols] + urecv[j // 2].astype(F32)).astype(BF16)
            upper_far.start()

    def third(j):
        cols = pl.ds(j * part, part)
        low_near[j, 0].wait_recv()
        low_far[j].wait_recv()
        total = up[mine, cols] + lrecv[j, 0].astype(F32) + lrecv2[j].astype(F32)
        fsend[cols, :] = total.T.astype(BF16)
        copy = remote(fsend.at[cols], frecv.at[cols], f_send.at[j], f_recv.at[j], (nxt, a))
        copy.start()
        final_out.append(copy)

    for j in range(na + 2):
        if j < na:
            compute(j)
        if 0 <= j - 1 < na:
            second(j - 1)
        if 0 <= j - 2 < na:
            third(j - 2)

    diag_far.wait_recv()
    out_ref[1] = (diag[:, mine] + drecv[x].astype(F32) + drecv2[...].astype(F32)) * scale

    remote(usend.at[0], urecv.at[x], u_send.at[0], u_recv.at[x], (b, near)).wait_recv()
    upper_far.wait_recv()
    out_ref[2] = (up[:, mine] + urecv[x].astype(F32) + urecv2[...].astype(F32)) * scale

    for j in range(na):
        final_out[j].wait_recv()
        cut = slice(j * part, (j + 1) * part)
        out_ref[0, cut] = frecv[cut].astype(F32) * scale

    for copy in (coef_out + half_out + list(gather_out.values()) + [diag_near, diag_far, upper_far]
                 + list(low_near.values()) + list(low_far.values()) + final_out):
        copy.wait_send()
    for j in range(na):
        @pl.when(core != j % 2)
        def _():
            upper_near(j).wait_send()


def body(n, na, ints3c, coef, tile_mask):
    ints = jnp.transpose(ints3c, (0, 2, 1, 3))
    aux_p, kk, rows, cols = ints.shape
    occ = coef.shape[1]
    part = rows // na
    scale = (na * aux_p * 3 * occ) ** (-0.5)
    dma = pltpu.SemaphoreType.DMA
    out = pl.pallas_call(
        functools.partial(kernel, n, na, scale),
        out_shape=jax.ShapeDtypeStruct((3, rows, part), F32),
        in_specs=[
            pl.BlockSpec(memory_space=pltpu.SMEM),
            pl.BlockSpec(memory_space=pltpu.HBM),
            pl.BlockSpec(memory_space=pltpu.HBM),
        ],
        out_specs=pl.BlockSpec(memory_space=pltpu.VMEM),
        scratch_shapes=[
            pltpu.VMEM((rows, occ), BF16),
            pltpu.VMEM((3, aux_p, rows, cols), BF16),
            pltpu.VMEM((2, rows, occ), BF16),
            pltpu.VMEM((3, rows, aux_p * occ), BF16),
            pltpu.VMEM((2, rows, aux_p * occ), BF16),
            pltpu.VMEM((rows, rows), F32),
            pltpu.VMEM((2, na // 2, rows, part), BF16),
            pltpu.VMEM((na // 2, rows, part), BF16),
            pltpu.VMEM((rows, part), BF16),
            pltpu.VMEM((rows, part), BF16),
            pltpu.VMEM((rows, rows), F32),
            pltpu.VMEM((na, rows, part), BF16),
            pltpu.VMEM((na // 2, rows, part), BF16),
            pltpu.VMEM((rows, part), BF16),
            pltpu.VMEM((rows, part), BF16),
            pltpu.VMEM((na, 2, part, part), BF16),
            pltpu.VMEM((na, part, part), BF16),
            pltpu.VMEM((na, part, part), BF16),
            pltpu.VMEM((rows, part), BF16),
            pltpu.VMEM((rows, part), BF16),
            dma, dma((3, aux_p)),
            dma((2,)), dma((2,)),
            dma((2, 3)), dma((2, 3)),
            dma((2, na)), dma((2, na)),
            dma((2,)), dma((2,)),
            dma((3,)), dma((3,)),
            dma((na, 3)), dma((na, 3)),
            dma((na,)), dma((na,)),
        ],
        compiler_params=pltpu.CompilerParams(
            collective_id=0, has_side_effects=True, vmem_limit_bytes=63 * 1024 * 1024),
        cost_estimate=pl.CostEstimate(
            flops=2 * rows * rows * occ * aux_p * 8, bytes_accessed=ints.size * 2 + rows * rows * 12,
            transcendentals=0),
    )(jnp.transpose(tile_mask, (1, 0, 2)), coef, ints)
    return jnp.transpose(out, (1, 0, 2))


def solution(mesh):
    placed = (P("aux", "blk", None, None), P("blk", None), P("blk", None, None))
    return jax.shard_map(
        functools.partial(body, mesh.shape["blk"], mesh.shape["aux"]),
        mesh=mesh, in_specs=placed, out_specs=P("blk", None, "aux"), check_vma=False,
    )
```

```python
import functools

import jax
import jax.numpy as jnp
from jax import lax
from jax.experimental import pallas as pl
from jax.experimental.pallas import tpu as pltpu
from jax.sharding import PartitionSpec as P

MESH = pl.DeviceIdType.MESH
F32 = jnp.float32
BF16 = jnp.bfloat16


def dot(a, b):
    return jnp.dot(a, b, preferred_element_type=F32)


def dot_t(a, b):
    return lax.dot_general(a, b, (((1,), (1,)), ((), ())), preferred_element_type=F32)


def kernel(n, na, scale, mask_ref, coef_ref, ints_ref, out_ref, coef_vmem, ints, cwin, hs, rh, diag, dsend, drecv,
           dsend2, drecv2, up, usend, urecv, usend2, urecv2, lrecv, lsend2, lrecv2, fsend, frecv, coef_sem, load_sem, c_send, c_recv, g_send, g_recv, h_send,
           h_recv, d_send, d_recv, u_send, u_recv, l_send, l_recv, f_send, f_recv):
    b = lax.axis_index("blk")
    a = lax.axis_index("aux")
    aux_p, _, rows, _ = ints_ref.shape
    occ = coef_ref.shape[1]
    tiles = mask_ref.shape[2]
    tile = rows // tiles
    part = rows // na
    nxt = lax.rem(b + 1, n)
    prv = lax.rem(b + n - 1, n)
    far = lax.rem(a + na // 2, na)
    near = a + 1 - 2 * lax.rem(a, 2)
    mates = [lax.rem(a + r, na) for r in range(1, na)]

    def remote(src, dst, ssem, rsem, to):
        return pltpu.make_async_remote_copy(
            src_ref=src, dst_ref=dst, send_sem=ssem, recv_sem=rsem, device_id=to, device_id_type=MESH)

    barrier = pltpu.get_barrier_semaphore()
    for to in [(nxt, a), (prv, a)] + [(b, m) for m in mates]:
        pl.semaphore_signal(barrier, inc=1, device_id=to, device_id_type=MESH)

    coef_load = pltpu.make_async_copy(coef_ref, coef_vmem, coef_sem)
    coef_load.start()
    loads = {}
    for k in (1, 0, 2):
        for p in range(aux_p):
            loads[k, p] = pltpu.make_async_copy(
                ints_ref.at[p, k], ints.at[k, p], load_sem.at[k, p])
            loads[k, p].start()

    def transform(k, window, t0, t1):
        for p in range(aux_p):
            if t0 == 0:
                loads[k, p].wait()
            prod = dot(ints[k, p, t0 * tile:t1 * tile, :], window[...])
            for t in range(t0, t1):
                weight = mask_ref[k, 0, t].astype(F32)
                piece = prod[(t - t0) * tile:(t - t0 + 1) * tile, :] * weight
                hs[k, t * tile:(t + 1) * tile, p * occ:(p + 1) * occ] = piece.astype(BF16)

    coef_load.wait()
    pl.semaphore_wait(barrier, 2 + len(mates))

    mine = pl.ds(pl.multiple_of(a * part, part), part)
    coef_out = []
    for side, to in ((0, (nxt, a)), (1, (prv, a))):
        copy = remote(coef_vmem.at[mine], cwin.at[side, mine], c_send.at[side], c_recv.at[side], to)
        copy.start()
        coef_out.append(copy)

    half_one = remote(hs.at[1], rh.at[1], h_send.at[1, 0], h_recv.at[1, 0], (prv, a))
    half_zero = []
    for j in range(na):
        cut = pl.ds(j * part, part)
        half_zero.append(remote(hs.at[0, cut], rh.at[0, cut], h_send.at[0, j], h_recv.at[0, j], (prv, a)))

    transform(1, coef_vmem, 0, tiles)

    gather_out = {}

    def pass_on(side, r, owner, to):
        cut = pl.ds(pl.multiple_of(owner * part, part), part)
        gather_out[side, r] = remote(cwin.at[side, cut], cwin.at[side, cut], g_send.at[side, r],
                                     g_recv.at[side, r], (b, to))
        gather_out[side, r].start()

    for side in (0, 1):
        coef_out[side].wait_recv()
        pass_on(side, 0, a, far)
        pass_on(side, 1, a, near)
    half_one.start()
    for side in (0, 1):
        gather_out[side, 0].wait_recv()
        pass_on(side, 2, far, near)

    def gathered(side):
        gather_out[side, 1].wait_recv()
        gather_out[side, 2].wait_recv()

    gathered(0)
    transform(0, cwin.at[0], 0, tiles)
    half_zero[0].start()
    gathered(1)
    transform(2, cwin.at[1], 0, tiles)

    near_far = lax.rem(near + na // 2, na)
    core, x, far_x = lax.rem(a, 2), a // 2, far // 2
    near_core = lax.rem(near, 2)
    far_cols = pl.ds(pl.multiple_of(far * part, part), part)

    diag[...] = dot_t(hs[0], hs[0]) + dot_t(hs[1], hs[1]) + dot_t(hs[2], hs[2])
    for c in range(na):
        dsend[c % 2, c // 2] = diag[:, c * part:(c + 1) * part].astype(BF16)
    diag_near = remote(dsend.at[near_core], drecv, d_send.at[0], d_recv.at[0], (b, near))
    diag_near.start()

    half_one.wait_send()
    half_zero[1].start()
    half_one.wait_recv()
    up[...] = dot_t(hs[2], rh[1])

    diag_near.wait_recv()
    dsend2[...] = (diag[:, far_cols] + drecv[far_x].astype(F32)).astype(BF16)
    diag_far = remote(dsend2, drecv2, d_send.at[1], d_recv.at[1], (b, far))
    diag_far.start()

    low_near, low_far, final_out = {}, {}, []

    def upper_near(j):
        return remote(usend.at[j], urecv.at[j // 2], u_send.at[j // 2], u_recv.at[j // 2], (b, near))

    upper_far = remote(usend2, urecv2, u_send.at[2], u_recv.at[2], (b, far))

    def compute(j):
        half_zero[j].wait_recv()
        cols = pl.ds(j * part, part)
        value = up[:, cols] + dot_t(hs[1], rh[0, cols, :])
        up[:, cols] = value
        usend[j] = value.astype(BF16)
        for i, owner in enumerate((near, near_far)):
            take = pl.ds(pl.multiple_of(owner * part, part), part)
            low_near[j, i] = remote(usend.at[j, take], lrecv.at[j, i], l_send.at[j, i],
                                    l_recv.at[j, i], (b, near))
            low_near[j, i].start()

        @pl.when(core != j % 2)
        def _():
            upper_near(j).start()

    def second(j):
        cols = pl.ds(j * part, part)
        low_near[j, 1].wait_recv()
        lsend2[j] = (up[far_cols, cols] + lrecv[j, 1].astype(F32)).astype(BF16)
        low_far[j] = remote(lsend2.at[j], lrecv2.at[j], l_send.at[j, 2], l_recv.at[j, 2], (b, far))
        low_far[j].start()

        @pl.when(far == j)
        def _():
            upper_near(j).wait_recv()
            usend2[...] = (up[:, cols] + urecv[j // 2].astype(F32)).astype(BF16)
            upper_far.start()

    def third(j):
        cols = pl.ds(j * part, part)
        low_near[j, 0].wait_recv()
        low_far[j].wait_recv()
        total = up[mine, cols] + lrecv[j, 0].astype(F32) + lrecv2[j].astype(F32)
        fsend[cols, :] = total.T.astype(BF16)
        copy = remote(fsend.at[cols], frecv.at[cols], f_send.at[j], f_recv.at[j], (nxt, a))
        copy.start()
        final_out.append(copy)

    for j in range(na):
        if j + 2 < na:
            half_zero[j].wait_send()
            half_zero[j + 2].start()
        compute(j)
        if j > 0:
            third(j - 1)
        second(j)
        if j == 0:
            diag_far.wait_recv()
            out_ref[1] = (diag[:, mine] + drecv[x].astype(F32) + drecv2[...].astype(F32)) * scale
    third(na - 1)

    remote(usend.at[0], urecv.at[x], u_send.at[0], u_recv.at[x], (b, near)).wait_recv()
    upper_far.wait_recv()
    out_ref[2] = (up[:, mine] + urecv[x].astype(F32) + urecv2[...].astype(F32)) * scale

    for j in range(na):
        final_out[j].wait_recv()
        cut = slice(j * part, (j + 1) * part)
        out_ref[0, cut] = frecv[cut].astype(F32) * scale

    for copy in (coef_out + half_zero[na - 2:] + list(gather_out.values()) + [diag_near, diag_far, upper_far]
                 + list(low_near.values()) + list(low_far.values()) + final_out):
        copy.wait_send()
    for j in range(na):
        @pl.when(core != j % 2)
        def _():
            upper_near(j).wait_send()


def body(n, na, ints3c, coef, tile_mask):
    ints = jnp.transpose(ints3c, (0, 2, 1, 3))
    aux_p, kk, rows, cols = ints.shape
    occ = coef.shape[1]
    part = rows // na
    scale = (na * aux_p * 3 * occ) ** (-0.5)
    dma = pltpu.SemaphoreType.DMA
    out = pl.pallas_call(
        functools.partial(kernel, n, na, scale),
        out_shape=jax.ShapeDtypeStruct((3, rows, part), F32),
        in_specs=[
            pl.BlockSpec(memory_space=pltpu.SMEM),
            pl.BlockSpec(memory_space=pltpu.HBM),
            pl.BlockSpec(memory_space=pltpu.HBM),
        ],
        out_specs=pl.BlockSpec(memory_space=pltpu.VMEM),
        scratch_shapes=[
            pltpu.VMEM((rows, occ), BF16),
            pltpu.VMEM((3, aux_p, rows, cols), BF16),
            pltpu.VMEM((2, rows, occ), BF16),
            pltpu.VMEM((3, rows, aux_p * occ), BF16),
            pltpu.VMEM((2, rows, aux_p * occ), BF16),
            pltpu.VMEM((rows, rows), F32),
            pltpu.VMEM((2, na // 2, rows, part), BF16),
            pltpu.VMEM((na // 2, rows, part), BF16),
            pltpu.VMEM((rows, part), BF16),
            pltpu.VMEM((rows, part), BF16),
            pltpu.VMEM((rows, rows), F32),
            pltpu.VMEM((na, rows, part), BF16),
            pltpu.VMEM((na // 2, rows, part), BF16),
            pltpu.VMEM((rows, part), BF16),
            pltpu.VMEM((rows, part), BF16),
            pltpu.VMEM((na, 2, part, part), BF16),
            pltpu.VMEM((na, part, part), BF16),
            pltpu.VMEM((na, part, part), BF16),
            pltpu.VMEM((rows, part), BF16),
            pltpu.VMEM((rows, part), BF16),
            dma, dma((3, aux_p)),
            dma((2,)), dma((2,)),
            dma((2, 3)), dma((2, 3)),
            dma((2, na)), dma((2, na)),
            dma((2,)), dma((2,)),
            dma((3,)), dma((3,)),
            dma((na, 3)), dma((na, 3)),
            dma((na,)), dma((na,)),
        ],
        compiler_params=pltpu.CompilerParams(
            collective_id=0, has_side_effects=True, vmem_limit_bytes=63 * 1024 * 1024),
        cost_estimate=pl.CostEstimate(
            flops=2 * rows * rows * occ * aux_p * 8, bytes_accessed=ints.size * 2 + rows * rows * 12,
            transcendentals=0),
    )(jnp.transpose(tile_mask, (1, 0, 2)), coef, ints)
    return jnp.transpose(out, (1, 0, 2))


def solution(mesh):
    placed = (P("aux", "blk", None, None), P("blk", None), P("blk", None, None))
    return jax.shard_map(
        functools.partial(body, mesh.shape["blk"], mesh.shape["aux"]),
        mesh=mesh, in_specs=placed, out_specs=P("blk", None, "aux"), check_vma=False,
    )
```

```python
import functools

import jax
import jax.numpy as jnp
from jax import lax
from jax.experimental import pallas as pl
from jax.experimental.pallas import tpu as pltpu
from jax.sharding import PartitionSpec as P

MESH = pl.DeviceIdType.MESH
F32 = jnp.float32
BF16 = jnp.bfloat16


def dot(a, b):
    return jnp.dot(a, b, preferred_element_type=F32)


def dot_t(a, b):
    return lax.dot_general(a, b, (((1,), (1,)), ((), ())), preferred_element_type=F32)


def kernel(n, na, scale, mask_ref, coef_ref, ints_ref, out_ref, coef_vmem, ints, cwin, hs, rh, diag, dsend, drecv,
           dsend2, drecv2, up, usend, urecv, usend2, urecv2, lrecv, lsend2, lrecv2, fsend, frecv, coef_sem, load_sem, c_send, c_recv, g_send, g_recv, h_send,
           h_recv, d_send, d_recv, u_send, u_recv, l_send, l_recv, f_send, f_recv):
    b = lax.axis_index("blk")
    a = lax.axis_index("aux")
    aux_p, _, rows, _ = ints_ref.shape
    occ = coef_ref.shape[1]
    tiles = mask_ref.shape[2]
    tile = rows // tiles
    part = rows // na
    nxt = lax.rem(b + 1, n)
    prv = lax.rem(b + n - 1, n)
    far = lax.rem(a + na // 2, na)
    near = a + 1 - 2 * lax.rem(a, 2)
    mates = [lax.rem(a + r, na) for r in range(1, na)]

    def remote(src, dst, ssem, rsem, to):
        return pltpu.make_async_remote_copy(
            src_ref=src, dst_ref=dst, send_sem=ssem, recv_sem=rsem, device_id=to, device_id_type=MESH)

    barrier = pltpu.get_barrier_semaphore()
    for to in [(nxt, a), (prv, a)] + [(b, m) for m in mates]:
        pl.semaphore_signal(barrier, inc=1, device_id=to, device_id_type=MESH)

    coef_load = pltpu.make_async_copy(coef_ref, coef_vmem, coef_sem)
    coef_load.start()
    loads = {}
    for k in (1, 0, 2):
        for p in range(aux_p):
            loads[k, p] = pltpu.make_async_copy(
                ints_ref.at[p, k], ints.at[k, p], load_sem.at[k, p])
            loads[k, p].start()

    def transform(k, window, t0, t1):
        for p in range(aux_p):
            if t0 == 0:
                loads[k, p].wait()
            prod = dot(ints[k, p, t0 * tile:t1 * tile, :], window[...])
            for t in range(t0, t1):
                weight = mask_ref[k, 0, t].astype(F32)
                piece = prod[(t - t0) * tile:(t - t0 + 1) * tile, :] * weight
                hs[k, t * tile:(t + 1) * tile, p * occ:(p + 1) * occ] = piece.astype(BF16)

    coef_load.wait()
    pl.semaphore_wait(barrier, 2 + len(mates))

    mine = pl.ds(pl.multiple_of(a * part, part), part)
    coef_out = []
    for side, to in ((0, (nxt, a)), (1, (prv, a))):
        copy = remote(coef_vmem.at[mine], cwin.at[side, mine], c_send.at[side], c_recv.at[side], to)
        copy.start()
        coef_out.append(copy)

    half_out = []

    def send_half(k, j):
        cut = pl.ds(j * part, part)
        copy = remote(hs.at[k, cut], rh.at[k, cut], h_send.at[k, j], h_recv.at[k, j], (prv, a))
        copy.start()
        half_out.append(copy)

    transform(1, coef_vmem, 0, tiles)
    send_half(1, 0)

    gather_out = {}

    def pass_on(side, r, owner, to):
        cut = pl.ds(pl.multiple_of(owner * part, part), part)
        gather_out[side, r] = remote(cwin.at[side, cut], cwin.at[side, cut], g_send.at[side, r],
                                     g_recv.at[side, r], (b, to))
        gather_out[side, r].start()

    for side in (0, 1):
        coef_out[side].wait_recv()
        pass_on(side, 0, a, far)
        pass_on(side, 1, a, near)
    for j in range(1, na):
        send_half(1, j)
    for side in (0, 1):
        gather_out[side, 0].wait_recv()
        pass_on(side, 2, far, near)

    def gathered(side):
        gather_out[side, 1].wait_recv()
        gather_out[side, 2].wait_recv()

    gathered(0)
    per = tiles // na
    for j in range(na):
        transform(0, cwin.at[0], j * per, (j + 1) * per)
        send_half(0, j)
    gathered(1)
    transform(2, cwin.at[1], 0, tiles)

    near_far = lax.rem(near + na // 2, na)
    core, x, far_x = lax.rem(a, 2), a // 2, far // 2
    near_core = lax.rem(near, 2)
    far_cols = pl.ds(pl.multiple_of(far * part, part), part)

    diag[...] = dot_t(hs[0], hs[0]) + dot_t(hs[1], hs[1]) + dot_t(hs[2], hs[2])
    for c in range(na):
        dsend[c % 2, c // 2] = diag[:, c * part:(c + 1) * part].astype(BF16)
    diag_near = remote(dsend.at[near_core], drecv, d_send.at[0], d_recv.at[0], (b, near))
    diag_near.start()

    for j in range(na):
        half_out[j].wait_recv()
    up[...] = dot_t(hs[2], rh[1])

    diag_near.wait_recv()
    dsend2[...] = (diag[:, far_cols] + drecv[far_x].astype(F32)).astype(BF16)
    diag_far = remote(dsend2, drecv2, d_send.at[1], d_recv.at[1], (b, far))
    diag_far.start()

    low_near, low_far, final_out = {}, {}, []

    def upper_near(j):
        return remote(usend.at[j], urecv.at[j // 2], u_send.at[j // 2], u_recv.at[j // 2], (b, near))

    upper_far = remote(usend2, urecv2, u_send.at[2], u_recv.at[2], (b, far))

    def compute(j):
        half_out[na + j].wait_recv()
        cols = pl.ds(j * part, part)
        value = up[:, cols] + dot_t(hs[1], rh[0, cols, :])
        up[:, cols] = value
        usend[j] = value.astype(BF16)
        for i, owner in enumerate((near, near_far)):
            take = pl.ds(pl.multiple_of(owner * part, part), part)
            low_near[j, i] = remote(usend.at[j, take], lrecv.at[j, i], l_send.at[j, i],
                                    l_recv.at[j, i], (b, near))
            low_near[j, i].start()

        @pl.when(core != j % 2)
        def _():
            upper_near(j).start()

    def second(j):
        cols = pl.ds(j * part, part)
        low_near[j, 1].wait_recv()
        lsend2[j] = (up[far_cols, cols] + lrecv[j, 1].astype(F32)).astype(BF16)
        low_far[j] = remote(lsend2.at[j], lrecv2.at[j], l_send.at[j, 2], l_recv.at[j, 2], (b, far))
        low_far[j].start()

        @pl.when(far == j)
        def _():
            upper_near(j).wait_recv()
            usend2[...] = (up[:, cols] + urecv[j // 2].astype(F32)).astype(BF16)
            upper_far.start()

    def third(j):
        cols = pl.ds(j * part, part)
        low_near[j, 0].wait_recv()
        low_far[j].wait_recv()
        total = up[mine, cols] + lrecv[j, 0].astype(F32) + lrecv2[j].astype(F32)
        fsend[cols, :] = total.T.astype(BF16)
        copy = remote(fsend.at[cols], frecv.at[cols], f_send.at[j], f_recv.at[j], (nxt, a))
        copy.start()
        final_out.append(copy)

    for j in range(na + 2):
        if j < na:
            compute(j)
        if 0 <= j - 1 < na:
            second(j - 1)
        if 0 <= j - 2 < na:
            third(j - 2)

    diag_far.wait_recv()
    out_ref[1] = (diag[:, mine] + drecv[x].astype(F32) + drecv2[...].astype(F32)) * scale

    remote(usend.at[0], urecv.at[x], u_send.at[0], u_recv.at[x], (b, near)).wait_recv()
    upper_far.wait_recv()
    out_ref[2] = (up[:, mine] + urecv[x].astype(F32) + urecv2[...].astype(F32)) * scale

    for j in range(na):
        final_out[j].wait_recv()
        cut = slice(j * part, (j + 1) * part)
        out_ref[0, cut] = frecv[cut].astype(F32) * scale

    for copy in (coef_out + half_out + list(gather_out.values()) + [diag_near, diag_far, upper_far]
                 + list(low_near.values()) + list(low_far.values()) + final_out):
        copy.wait_send()
    for j in range(na):
        @pl.when(core != j % 2)
        def _():
            upper_near(j).wait_send()


def move(pieces, src_ref, dst_ref, sem):
    rows = src_ref.shape[1] // pieces
    copies = []
    for d in range(src_ref.shape[0]):
        for i in range(pieces):
            cut = pl.ds(i * rows, rows)
            copies.append(pltpu.make_async_copy(src_ref.at[d, cut], dst_ref.at[d, cut], sem.at[d, i]))
            copies[-1].start()
    for copy in copies:
        copy.wait()


def body(n, na, ints3c, coef, tile_mask):
    ints = jnp.transpose(ints3c, (0, 2, 1, 3))
    aux_p, kk, rows, cols = ints.shape
    occ = coef.shape[1]
    part = rows // na
    scale = (na * aux_p * 3 * occ) ** (-0.5)
    dma = pltpu.SemaphoreType.DMA
    out = pl.pallas_call(
        functools.partial(kernel, n, na, scale),
        out_shape=jax.ShapeDtypeStruct((3, rows, part), F32),
        in_specs=[
            pl.BlockSpec(memory_space=pltpu.SMEM),
            pl.BlockSpec(memory_space=pltpu.HBM),
            pl.BlockSpec(memory_space=pltpu.HBM),
        ],
        out_specs=pl.BlockSpec(memory_space=pltpu.VMEM),
        scratch_shapes=[
            pltpu.VMEM((rows, occ), BF16),
            pltpu.VMEM((3, aux_p, rows, cols), BF16),
            pltpu.VMEM((2, rows, occ), BF16),
            pltpu.VMEM((3, rows, aux_p * occ), BF16),
            pltpu.VMEM((2, rows, aux_p * occ), BF16),
            pltpu.VMEM((rows, rows), F32),
            pltpu.VMEM((2, na // 2, rows, part), BF16),
            pltpu.VMEM((na // 2, rows, part), BF16),
            pltpu.VMEM((rows, part), BF16),
            pltpu.VMEM((rows, part), BF16),
            pltpu.VMEM((rows, rows), F32),
            pltpu.VMEM((na, rows, part), BF16),
            pltpu.VMEM((na // 2, rows, part), BF16),
            pltpu.VMEM((rows, part), BF16),
            pltpu.VMEM((rows, part), BF16),
            pltpu.VMEM((na, 2, part, part), BF16),
            pltpu.VMEM((na, part, part), BF16),
            pltpu.VMEM((na, part, part), BF16),
            pltpu.VMEM((rows, part), BF16),
            pltpu.VMEM((rows, part), BF16),
            dma, dma((3, aux_p)),
            dma((2,)), dma((2,)),
            dma((2, 3)), dma((2, 3)),
            dma((2, na)), dma((2, na)),
            dma((2,)), dma((2,)),
            dma((3,)), dma((3,)),
            dma((na, 3)), dma((na, 3)),
            dma((na,)), dma((na,)),
        ],
        compiler_params=pltpu.CompilerParams(
            collective_id=0, has_side_effects=True, vmem_limit_bytes=63 * 1024 * 1024),
        cost_estimate=pl.CostEstimate(
            flops=2 * rows * rows * occ * aux_p * 8, bytes_accessed=ints.size * 2 + rows * rows * 12,
            transcendentals=0),
    )(jnp.transpose(tile_mask, (1, 0, 2)), coef, ints)
    out = pl.pallas_call(
        functools.partial(move, 4),
        out_shape=jax.ShapeDtypeStruct(out.shape, out.dtype),
        in_specs=[pl.BlockSpec(memory_space=pl.ANY)],
        out_specs=pl.BlockSpec(memory_space=pl.ANY),
        scratch_shapes=[dma((3, 4))],
    )(out)
    return jnp.transpose(out, (1, 0, 2))


def solution(mesh):
    placed = (P("aux", "blk", None, None), P("blk", None), P("blk", None, None))
    return jax.shard_map(
        functools.partial(body, mesh.shape["blk"], mesh.shape["aux"]),
        mesh=mesh, in_specs=placed, out_specs=P("blk", None, "aux"), check_vma=False,
    )
```

```python
import functools

import jax
import jax.numpy as jnp
from jax import lax
from jax.experimental import pallas as pl
from jax.experimental.pallas import tpu as pltpu
from jax.sharding import PartitionSpec as P

MESH = pl.DeviceIdType.MESH
F32 = jnp.float32
BF16 = jnp.bfloat16


def dot(a, b):
    return jnp.dot(a, b, preferred_element_type=F32)


def dot_t(a, b):
    return lax.dot_general(a, b, (((1,), (1,)), ((), ())), preferred_element_type=F32)


def kernel(n, na, scale, mask_ref, coef_ref, ints_ref, out_ref, coef_vmem, ints, cwin, hs, rh, diag, dsend, drecv,
           dsend2, drecv2, up, usend, urecv, usend2, urecv2, lrecv, lsend2, lrecv2, fsend, frecv, coef_sem, load_sem, c_send, c_recv, g_send, g_recv, h_send,
           h_recv, d_send, d_recv, u_send, u_recv, l_send, l_recv, f_send, f_recv):
    b = lax.axis_index("blk")
    a = lax.axis_index("aux")
    aux_p, _, rows, _ = ints_ref.shape
    occ = coef_ref.shape[1]
    tiles = mask_ref.shape[2]
    tile = rows // tiles
    part = rows // na
    nxt = lax.rem(b + 1, n)
    prv = lax.rem(b + n - 1, n)
    far = lax.rem(a + na // 2, na)
    near = a + 1 - 2 * lax.rem(a, 2)
    mates = [lax.rem(a + r, na) for r in range(1, na)]

    def remote(src, dst, ssem, rsem, to):
        return pltpu.make_async_remote_copy(
            src_ref=src, dst_ref=dst, send_sem=ssem, recv_sem=rsem, device_id=to, device_id_type=MESH)

    barrier = pltpu.get_barrier_semaphore()
    for to in [(nxt, a), (prv, a)] + [(b, m) for m in mates]:
        pl.semaphore_signal(barrier, inc=1, device_id=to, device_id_type=MESH)

    coef_load = pltpu.make_async_copy(coef_ref, coef_vmem, coef_sem)
    coef_load.start()
    loads = {}
    for k in (1, 0, 2):
        for p in range(aux_p):
            loads[k, p] = pltpu.make_async_copy(
                ints_ref.at[p, k], ints.at[k, p], load_sem.at[k, p])
            loads[k, p].start()

    def transform(k, window, t0, t1):
        for p in range(aux_p):
            if t0 == 0:
                loads[k, p].wait()
            prod = dot(ints[k, p, t0 * tile:t1 * tile, :], window[...])
            for t in range(t0, t1):
                weight = mask_ref[k, 0, t].astype(F32)
                piece = prod[(t - t0) * tile:(t - t0 + 1) * tile, :] * weight
                hs[k, t * tile:(t + 1) * tile, p * occ:(p + 1) * occ] = piece.astype(BF16)

    coef_load.wait()
    pl.semaphore_wait(barrier, 2 + len(mates))

    mine = pl.ds(pl.multiple_of(a * part, part), part)
    coef_out = []
    for side, to in ((0, (nxt, a)), (1, (prv, a))):
        copy = remote(coef_vmem.at[mine], cwin.at[side, mine], c_send.at[side], c_recv.at[side], to)
        copy.start()
        coef_out.append(copy)

    half_out = []

    def send_half(k, j):
        cut = pl.ds(j * part, part)
        copy = remote(hs.at[k, cut], rh.at[k, cut], h_send.at[k, j], h_recv.at[k, j], (prv, a))
        copy.start()
        half_out.append(copy)

    transform(1, coef_vmem, 0, tiles)

    gather_out = {}

    def pass_on(side, r, owner, to):
        cut = pl.ds(pl.multiple_of(owner * part, part), part)
        gather_out[side, r] = remote(cwin.at[side, cut], cwin.at[side, cut], g_send.at[side, r],
                                     g_recv.at[side, r], (b, to))
        gather_out[side, r].start()

    for side in (0, 1):
        coef_out[side].wait_recv()
        pass_on(side, 0, a, far)
        pass_on(side, 1, a, near)
    for j in range(na):
        send_half(1, j)
    for side in (0, 1):
        gather_out[side, 0].wait_recv()
        pass_on(side, 2, far, near)

    def gathered(side):
        gather_out[side, 1].wait_recv()
        gather_out[side, 2].wait_recv()

    gathered(0)
    per = tiles // na
    for j in range(na):
        transform(0, cwin.at[0], j * per, (j + 1) * per)
        send_half(0, j)
    gathered(1)
    transform(2, cwin.at[1], 0, tiles)

    near_far = lax.rem(near + na // 2, na)
    core, x, far_x = lax.rem(a, 2), a // 2, far // 2
    near_core = lax.rem(near, 2)
    far_cols = pl.ds(pl.multiple_of(far * part, part), part)

    diag[...] = dot_t(hs[0], hs[0]) + dot_t(hs[1], hs[1]) + dot_t(hs[2], hs[2])
    for c in range(na):
        dsend[c % 2, c // 2] = diag[:, c * part:(c + 1) * part].astype(BF16)
    diag_near = remote(dsend.at[near_core], drecv, d_send.at[0], d_recv.at[0], (b, near))
    diag_near.start()

    for j in range(na):
        half_out[j].wait_recv()
    up[...] = dot_t(hs[2], rh[1])

    diag_near.wait_recv()
    dsend2[...] = (diag[:, far_cols] + drecv[far_x].astype(F32)).astype(BF16)
    diag_far = remote(dsend2, drecv2, d_send.at[1], d_recv.at[1], (b, far))
    diag_far.start()

    low_near, low_far, final_out = {}, {}, []

    def upper_near(j):
        return remote(usend.at[j], urecv.at[j // 2], u_send.at[j // 2], u_recv.at[j // 2], (b, near))

    upper_far = remote(usend2, urecv2, u_send.at[2], u_recv.at[2], (b, far))

    def compute(j):
        half_out[na + j].wait_recv()
        cols = pl.ds(j * part, part)
        value = up[:, cols] + dot_t(hs[1], rh[0, cols, :])
        up[:, cols] = value
        usend[j] = value.astype(BF16)
        for i, owner in enumerate((near, near_far)):
            take = pl.ds(pl.multiple_of(owner * part, part), part)
            low_near[j, i] = remote(usend.at[j, take], lrecv.at[j, i], l_send.at[j, i],
                                    l_recv.at[j, i], (b, near))
            low_near[j, i].start()

        @pl.when(core != j % 2)
        def _():
            upper_near(j).start()

    def second(j):
        cols = pl.ds(j * part, part)
        low_near[j, 1].wait_recv()
        lsend2[j] = (up[far_cols, cols] + lrecv[j, 1].astype(F32)).astype(BF16)
        low_far[j] = remote(lsend2.at[j], lrecv2.at[j], l_send.at[j, 2], l_recv.at[j, 2], (b, far))
        low_far[j].start()

        @pl.when(far == j)
        def _():
            upper_near(j).wait_recv()
            usend2[...] = (up[:, cols] + urecv[j // 2].astype(F32)).astype(BF16)
            upper_far.start()

    def third(j):
        cols = pl.ds(j * part, part)
        low_near[j, 0].wait_recv()
        low_far[j].wait_recv()
        total = up[mine, cols] + lrecv[j, 0].astype(F32) + lrecv2[j].astype(F32)
        fsend[cols, :] = total.T.astype(BF16)
        copy = remote(fsend.at[cols], frecv.at[cols], f_send.at[j], f_recv.at[j], (nxt, a))
        copy.start()
        final_out.append(copy)

    for j in range(na + 2):
        if j < na:
            compute(j)
        if 0 <= j - 1 < na:
            second(j - 1)
        if 0 <= j - 2 < na:
            third(j - 2)

    diag_far.wait_recv()
    out_ref[1] = (diag[:, mine] + drecv[x].astype(F32) + drecv2[...].astype(F32)) * scale

    remote(usend.at[0], urecv.at[x], u_send.at[0], u_recv.at[x], (b, near)).wait_recv()
    upper_far.wait_recv()
    out_ref[2] = (up[:, mine] + urecv[x].astype(F32) + urecv2[...].astype(F32)) * scale

    for j in range(na):
        final_out[j].wait_recv()
        cut = slice(j * part, (j + 1) * part)
        out_ref[0, cut] = frecv[cut].astype(F32) * scale

    for copy in (coef_out + half_out + list(gather_out.values()) + [diag_near, diag_far, upper_far]
                 + list(low_near.values()) + list(low_far.values()) + final_out):
        copy.wait_send()
    for j in range(na):
        @pl.when(core != j % 2)
        def _():
            upper_near(j).wait_send()


def move(src_ref, dst_ref, held, in_sem, out_sem):
    blocks = src_ref.shape[0]
    into = [pltpu.make_async_copy(src_ref.at[d], held.at[d], in_sem.at[d]) for d in range(blocks)]
    back = [pltpu.make_async_copy(held.at[d], dst_ref.at[d], out_sem.at[d]) for d in range(blocks)]
    for copy in into:
        copy.start()
    for d in range(blocks):
        into[d].wait()
        back[d].start()
    for copy in back:
        copy.wait()


def body(n, na, ints3c, coef, tile_mask):
    ints = jnp.transpose(ints3c, (0, 2, 1, 3))
    aux_p, kk, rows, cols = ints.shape
    occ = coef.shape[1]
    part = rows // na
    scale = (na * aux_p * 3 * occ) ** (-0.5)
    dma = pltpu.SemaphoreType.DMA
    out = pl.pallas_call(
        functools.partial(kernel, n, na, scale),
        out_shape=jax.ShapeDtypeStruct((3, rows, part), F32),
        in_specs=[
            pl.BlockSpec(memory_space=pltpu.SMEM),
            pl.BlockSpec(memory_space=pltpu.HBM),
            pl.BlockSpec(memory_space=pltpu.HBM),
        ],
        out_specs=pl.BlockSpec(memory_space=pltpu.VMEM),
        scratch_shapes=[
            pltpu.VMEM((rows, occ), BF16),
            pltpu.VMEM((3, aux_p, rows, cols), BF16),
            pltpu.VMEM((2, rows, occ), BF16),
            pltpu.VMEM((3, rows, aux_p * occ), BF16),
            pltpu.VMEM((2, rows, aux_p * occ), BF16),
            pltpu.VMEM((rows, rows), F32),
            pltpu.VMEM((2, na // 2, rows, part), BF16),
            pltpu.VMEM((na // 2, rows, part), BF16),
            pltpu.VMEM((rows, part), BF16),
            pltpu.VMEM((rows, part), BF16),
            pltpu.VMEM((rows, rows), F32),
            pltpu.VMEM((na, rows, part), BF16),
            pltpu.VMEM((na // 2, rows, part), BF16),
            pltpu.VMEM((rows, part), BF16),
            pltpu.VMEM((rows, part), BF16),
            pltpu.VMEM((na, 2, part, part), BF16),
            pltpu.VMEM((na, part, part), BF16),
            pltpu.VMEM((na, part, part), BF16),
            pltpu.VMEM((rows, part), BF16),
            pltpu.VMEM((rows, part), BF16),
            dma, dma((3, aux_p)),
            dma((2,)), dma((2,)),
            dma((2, 3)), dma((2, 3)),
            dma((2, na)), dma((2, na)),
            dma((2,)), dma((2,)),
            dma((3,)), dma((3,)),
            dma((na, 3)), dma((na, 3)),
            dma((na,)), dma((na,)),
        ],
        compiler_params=pltpu.CompilerParams(
            collective_id=0, has_side_effects=True, vmem_limit_bytes=63 * 1024 * 1024),
        cost_estimate=pl.CostEstimate(
            flops=2 * rows * rows * occ * aux_p * 8, bytes_accessed=ints.size * 2 + rows * rows * 12,
            transcendentals=0),
    )(jnp.transpose(tile_mask, (1, 0, 2)), coef, ints)
    out = pl.pallas_call(
        move,
        out_shape=jax.ShapeDtypeStruct(out.shape, out.dtype),
        in_specs=[pl.BlockSpec(memory_space=pl.ANY)],
        out_specs=pl.BlockSpec(memory_space=pl.ANY),
        scratch_shapes=[pltpu.VMEM(out.shape, out.dtype), dma((3,)), dma((3,))],
        compiler_params=pltpu.CompilerParams(vmem_limit_bytes=63 * 1024 * 1024),
    )(out)
    return jnp.transpose(out, (1, 0, 2))


def solution(mesh):
    placed = (P("aux", "blk", None, None), P("blk", None), P("blk", None, None))
    return jax.shard_map(
        functools.partial(body, mesh.shape["blk"], mesh.shape["aux"]),
        mesh=mesh, in_specs=placed, out_specs=P("blk", None, "aux"), check_vma=False,
    )
```

```python
import functools

import jax
import jax.numpy as jnp
from jax import lax
from jax.experimental import pallas as pl
from jax.experimental.pallas import tpu as pltpu
from jax.sharding import PartitionSpec as P

MESH = pl.DeviceIdType.MESH
F32 = jnp.float32
BF16 = jnp.bfloat16


def dot(a, b):
    return jnp.dot(a, b, preferred_element_type=F32)


def dot_t(a, b):
    return lax.dot_general(a, b, (((1,), (1,)), ((), ())), preferred_element_type=F32)


def kernel(n, na, scale, mask_ref, coef_ref, ints_ref, out_ref, coef_vmem, ints, cwin, hs, rh, diag, dsend, drecv,
           dsend2, drecv2, up, usend, urecv, usend2, urecv2, lrecv, lsend2, lrecv2, fsend, frecv, coef_sem, load_sem, c_send, c_recv, g_send, g_recv, h_send,
           h_recv, d_send, d_recv, u_send, u_recv, l_send, l_recv, f_send, f_recv):
    b = lax.axis_index("blk")
    a = lax.axis_index("aux")
    aux_p, _, rows, _ = ints_ref.shape
    occ = coef_ref.shape[1]
    tiles = mask_ref.shape[2]
    tile = rows // tiles
    part = rows // na
    nxt = lax.rem(b + 1, n)
    prv = lax.rem(b + n - 1, n)
    far = lax.rem(a + na // 2, na)
    near = a + 1 - 2 * lax.rem(a, 2)
    mates = [lax.rem(a + r, na) for r in range(1, na)]

    def remote(src, dst, ssem, rsem, to):
        return pltpu.make_async_remote_copy(
            src_ref=src, dst_ref=dst, send_sem=ssem, recv_sem=rsem, device_id=to, device_id_type=MESH)

    barrier = pltpu.get_barrier_semaphore()
    for to in [(nxt, a), (prv, a)] + [(b, m) for m in mates]:
        pl.semaphore_signal(barrier, inc=1, device_id=to, device_id_type=MESH)

    coef_load = pltpu.make_async_copy(coef_ref, coef_vmem, coef_sem)
    coef_load.start()
    loads = {}
    for k in (1, 0, 2):
        for p in range(aux_p):
            loads[k, p] = pltpu.make_async_copy(
                ints_ref.at[p, k], ints.at[k, p], load_sem.at[k, p])
            loads[k, p].start()

    def transform(k, window, t0, t1):
        for p in range(aux_p):
            if t0 == 0:
                loads[k, p].wait()
            prod = dot(ints[k, p, t0 * tile:t1 * tile, :], window[...])
            for t in range(t0, t1):
                weight = mask_ref[k, 0, t].astype(F32)
                piece = prod[(t - t0) * tile:(t - t0 + 1) * tile, :] * weight
                hs[k, t * tile:(t + 1) * tile, p * occ:(p + 1) * occ] = piece.astype(BF16)

    coef_load.wait()
    pl.semaphore_wait(barrier, 2 + len(mates))

    mine = pl.ds(pl.multiple_of(a * part, part), part)
    coef_out = []
    for side, to in ((0, (nxt, a)), (1, (prv, a))):
        copy = remote(coef_vmem.at[mine], cwin.at[side, mine], c_send.at[side], c_recv.at[side], to)
        copy.start()
        coef_out.append(copy)

    half_out = []

    def send_half(k, j):
        cut = pl.ds(j * part, part)
        copy = remote(hs.at[k, cut], rh.at[k, cut], h_send.at[k, j], h_recv.at[k, j], (prv, a))
        copy.start()
        half_out.append(copy)

    transform(1, coef_vmem, 0, tiles)

    gather_out = {}

    def pass_on(side, r, owner, to):
        cut = pl.ds(pl.multiple_of(owner * part, part), part)
        gather_out[side, r] = remote(cwin.at[side, cut], cwin.at[side, cut], g_send.at[side, r],
                                     g_recv.at[side, r], (b, to))
        gather_out[side, r].start()

    for side in (0, 1):
        coef_out[side].wait_recv()
        pass_on(side, 0, a, far)
        pass_on(side, 1, a, near)
    half_one = remote(hs.at[1], rh.at[1], h_send.at[1, 0], h_recv.at[1, 0], (prv, a))
    half_one.start()
    for side in (0, 1):
        gather_out[side, 0].wait_recv()
        pass_on(side, 2, far, near)

    def gathered(side):
        gather_out[side, 1].wait_recv()
        gather_out[side, 2].wait_recv()

    gathered(0)
    per = tiles // na
    for j in range(na):
        transform(0, cwin.at[0], j * per, (j + 1) * per)
        send_half(0, j)
    gathered(1)
    transform(2, cwin.at[1], 0, tiles)

    near_far = lax.rem(near + na // 2, na)
    core, x, far_x = lax.rem(a, 2), a // 2, far // 2
    near_core = lax.rem(near, 2)
    far_cols = pl.ds(pl.multiple_of(far * part, part), part)

    diag[...] = dot_t(hs[0], hs[0]) + dot_t(hs[1], hs[1]) + dot_t(hs[2], hs[2])
    for c in range(na):
        dsend[c % 2, c // 2] = diag[:, c * part:(c + 1) * part].astype(BF16)
    diag_near = remote(dsend.at[near_core], drecv, d_send.at[0], d_recv.at[0], (b, near))
    diag_near.start()

    half_one.wait_recv()
    up[...] = dot_t(hs[2], rh[1])

    diag_near.wait_recv()
    dsend2[...] = (diag[:, far_cols] + drecv[far_x].astype(F32)).astype(BF16)
    diag_far = remote(dsend2, drecv2, d_send.at[1], d_recv.at[1], (b, far))
    diag_far.start()

    low_near, low_far, final_out = {}, {}, []

    def upper_near(j):
        return remote(usend.at[j], urecv.at[j // 2], u_send.at[j // 2], u_recv.at[j // 2], (b, near))

    upper_far = remote(usend2, urecv2, u_send.at[2], u_recv.at[2], (b, far))

    def compute(j):
        half_out[j].wait_recv()
        cols = pl.ds(j * part, part)
        value = up[:, cols] + dot_t(hs[1], rh[0, cols, :])
        up[:, cols] = value
        usend[j] = value.astype(BF16)
        for i, owner in enumerate((near, near_far)):
            take = pl.ds(pl.multiple_of(owner * part, part), part)
            low_near[j, i] = remote(usend.at[j, take], lrecv.at[j, i], l_send.at[j, i],
                                    l_recv.at[j, i], (b, near))
            low_near[j, i].start()

        @pl.when(core != j % 2)
        def _():
            upper_near(j).start()

    def second(j):
        cols = pl.ds(j * part, part)
        low_near[j, 1].wait_recv()
        lsend2[j] = (up[far_cols, cols] + lrecv[j, 1].astype(F32)).astype(BF16)
        low_far[j] = remote(lsend2.at[j], lrecv2.at[j], l_send.at[j, 2], l_recv.at[j, 2], (b, far))
        low_far[j].start()

        @pl.when(far == j)
        def _():
            upper_near(j).wait_recv()
            usend2[...] = (up[:, cols] + urecv[j // 2].astype(F32)).astype(BF16)
            upper_far.start()

    def third(j):
        cols = pl.ds(j * part, part)
        low_near[j, 0].wait_recv()
        low_far[j].wait_recv()
        total = up[mine, cols] + lrecv[j, 0].astype(F32) + lrecv2[j].astype(F32)
        fsend[cols, :] = total.T.astype(BF16)
        copy = remote(fsend.at[cols], frecv.at[cols], f_send.at[j], f_recv.at[j], (nxt, a))
        copy.start()
        final_out.append(copy)

    for j in range(na + 2):
        if j < na:
            compute(j)
        if 0 <= j - 1 < na:
            second(j - 1)
        if 0 <= j - 2 < na:
            third(j - 2)
        if j == 1:
            diag_far.wait_recv()
            out_ref[1] = (diag[:, mine] + drecv[x].astype(F32) + drecv2[...].astype(F32)) * scale

    remote(usend.at[0], urecv.at[x], u_send.at[0], u_recv.at[x], (b, near)).wait_recv()
    upper_far.wait_recv()
    out_ref[2] = (up[:, mine] + urecv[x].astype(F32) + urecv2[...].astype(F32)) * scale

    for j in range(na):
        final_out[j].wait_recv()
        cut = slice(j * part, (j + 1) * part)
        out_ref[0, cut] = frecv[cut].astype(F32) * scale

    for copy in (coef_out + [half_one] + half_out + list(gather_out.values()) + [diag_near, diag_far, upper_far]
                 + list(low_near.values()) + list(low_far.values()) + final_out):
        copy.wait_send()
    for j in range(na):
        @pl.when(core != j % 2)
        def _():
            upper_near(j).wait_send()


def body(n, na, ints3c, coef, tile_mask):
    ints = jnp.transpose(ints3c, (0, 2, 1, 3))
    aux_p, kk, rows, cols = ints.shape
    occ = coef.shape[1]
    part = rows // na
    scale = (na * aux_p * 3 * occ) ** (-0.5)
    dma = pltpu.SemaphoreType.DMA
    out = pl.pallas_call(
        functools.partial(kernel, n, na, scale),
        out_shape=jax.ShapeDtypeStruct((3, rows, part), F32),
        in_specs=[
            pl.BlockSpec(memory_space=pltpu.SMEM),
            pl.BlockSpec(memory_space=pltpu.HBM),
            pl.BlockSpec(memory_space=pltpu.HBM),
        ],
        out_specs=pl.BlockSpec(memory_space=pltpu.VMEM),
        scratch_shapes=[
            pltpu.VMEM((rows, occ), BF16),
            pltpu.VMEM((3, aux_p, rows, cols), BF16),
            pltpu.VMEM((2, rows, occ), BF16),
            pltpu.VMEM((3, rows, aux_p * occ), BF16),
            pltpu.VMEM((2, rows, aux_p * occ), BF16),
            pltpu.VMEM((rows, rows), F32),
            pltpu.VMEM((2, na // 2, rows, part), BF16),
            pltpu.VMEM((na // 2, rows, part), BF16),
            pltpu.VMEM((rows, part), BF16),
            pltpu.VMEM((rows, part), BF16),
            pltpu.VMEM((rows, rows), F32),
            pltpu.VMEM((na, rows, part), BF16),
            pltpu.VMEM((na // 2, rows, part), BF16),
            pltpu.VMEM((rows, part), BF16),
            pltpu.VMEM((rows, part), BF16),
            pltpu.VMEM((na, 2, part, part), BF16),
            pltpu.VMEM((na, part, part), BF16),
            pltpu.VMEM((na, part, part), BF16),
            pltpu.VMEM((rows, part), BF16),
            pltpu.VMEM((rows, part), BF16),
            dma, dma((3, aux_p)),
            dma((2,)), dma((2,)),
            dma((2, 3)), dma((2, 3)),
            dma((2, na)), dma((2, na)),
            dma((2,)), dma((2,)),
            dma((3,)), dma((3,)),
            dma((na, 3)), dma((na, 3)),
            dma((na,)), dma((na,)),
        ],
        compiler_params=pltpu.CompilerParams(
            collective_id=0, has_side_effects=True, vmem_limit_bytes=63 * 1024 * 1024),
        cost_estimate=pl.CostEstimate(
            flops=2 * rows * rows * occ * aux_p * 8, bytes_accessed=ints.size * 2 + rows * rows * 12,
            transcendentals=0),
    )(jnp.transpose(tile_mask, (1, 0, 2)), coef, ints)
    return jnp.transpose(out, (1, 0, 2))


def solution(mesh):
    placed = (P("aux", "blk", None, None), P("blk", None), P("blk", None, None))
    return jax.shard_map(
        functools.partial(body, mesh.shape["blk"], mesh.shape["aux"]),
        mesh=mesh, in_specs=placed, out_specs=P("blk", None, "aux"), check_vma=False,
    )
```
